1024 devices in a mesh: group: 64 (over z, core), slot: 16 (over y, x).
Axes of the slice: x: 4, y: 4, z: 32, core: 2. Of those that a mesh axis runs over, the one named last changes fastest.
Arguments:
- tokens: bfloat16 [8192, 7168], P('group', 'slot'), may hold values from -620 to 620, as said below
- norm_gain: float32 [7168], P('slot'), may hold values from 0.1 to 1.9
- route_expert: int32 [8192, 2], P('group'), may hold values from 0 to 63, all different within a row; in each aligned block of 128 rows (0 to 127, 128 to 255, ...) at most 8 rows name the same one
- route_gate: bfloat16 [8192, 2], P('group'), may hold values from 0.29882812 to 2.5
- w_gate_up: bfloat16 [64, 7168, 2048], P('group', 'slot'), may hold values from -0.0625 to 0.0625
- w_down: bfloat16 [64, 1024, 7168], P('group', None, 'slot'), may hold values from -0.1875 to 0.1875
Outputs:
- mixed: bfloat16 [8192, 7168], P('group', 'slot')
The draws below stay inside these ranges and needn't reach their ends.
Inputs may be any that keep to these rules, and one draw needn't show every extreme that they name: `route_expert`: in the 128 rows of one group block no expert is named more than 8 times, a bound that some block reaches; a token's 2 experts differ. `tokens`: token rows; every row and column of order one up to a scale.
All inputs are finite; a program needn't handle non-finite values.
Results may differ from the reference program's by a relative error of at most 0.029.
Values may be sent and summed in bfloat16 or wider, within the bound.
No kernel may reach another device: no remote copies, remote signals or barrier semaphores. Data moves between devices by JAX's collectives and lax.ppermute only.
A program may use at most 32 MiB of HBM per device.

```python
import math
import jax
import jax.numpy as jnp
import numpy as np
from jax import lax

D = 7168
FF_E = 1024
TOPK_IN = 2
TOK_GRP = 128
EXPERTS = 64
CAP = 8
TOKENS = 8192
N_GROUP = 64
N_SLOT = 16


def draw_tokens(key, part):
    key = jax.random.fold_in(key, 11)
    key_base, key_cols, key_rows = jax.random.split(key, 3)
    position = jnp.arange(D, dtype=jnp.float32) / D
    row_scale = jnp.exp(jax.random.uniform(key_rows, (TOKENS, 1), jnp.float32, 0.0, math.log(10.0)))
    col_random = jnp.exp(jax.random.uniform(key_cols, (D,), jnp.float32, 0.0, math.log(3.4)))
    base = jnp.clip(jax.random.normal(key_base, (TOKENS, D), jnp.float32), -6.0, 6.0)
    col_scale = col_random * jnp.exp(position * math.log(3.0))
    return (base * row_scale * col_scale[None, :]).astype(jnp.bfloat16)


def block_levels(rng, shape, shards, least, top_value):
    def one(dim, shards_of):
        steps = jax.random.uniform(jax.random.fold_in(jax.random.fold_in(rng, 6), dim), (shards_of,), jnp.float32, least / len(shards), top_value / len(shards))
        return jnp.repeat(jnp.exp(steps), shape[dim] // shards_of).reshape((-1,) + (1,) * (len(shape) - dim - 1))

    level = one(*shards[0])
    for cut in shards[1:]:
        level = level * one(*cut)
    return level


def routed_block(key, own, number, rows, amount, top, bound, skew):
    order = jax.random.permutation(key, amount)
    heavy_load, common = portions_of(amount, rows * top, bound, skew, True), portions_of(amount, rows * top, bound, skew, False)
    places = jnp.arange(amount)

    def named(lengths, turn):
        used = int((lengths > 0).sum())
        fixed = max(1, used // 4)
        moved = fixed + (places - fixed + turn * (used - fixed)) % max(1, amount - fixed)
        return jnp.zeros((amount,), jnp.int32).at[order[jnp.where(places < fixed, places, moved)]].set(jnp.asarray(lengths, jnp.int32))

    lengths = jnp.where(number % 4 == 0, named(heavy_load, number // 4), named(common, number - number // 4 - 1))
    mixed = jax.random.permutation(jax.random.fold_in(own, 3), amount)
    source_of, sink = mixed[0:amount // 2 * 2:2], mixed[1:amount // 2 * 2:2]
    slack = jnp.minimum(lengths[source_of] - 1, bound - lengths[sink]) // 2
    slack = jnp.where((source_of == order[0]) | (sink == order[0]) | (lengths[sink] == 0), 0, jnp.maximum(slack, 0))
    moved = jax.random.randint(jax.random.fold_in(own, 4), (amount // 2,), 0, 1 << 20) % (slack + 1)
    lengths = lengths.at[source_of].add(-moved).at[sink].add(moved)
    items = jnp.searchsorted(jnp.cumsum(lengths), jnp.arange(rows * top), side="right").astype(jnp.int32)
    listing = items.reshape(top, rows).T
    listing = listing[jax.random.permutation(jax.random.fold_in(own, 1), rows)]
    turn = jax.random.randint(jax.random.fold_in(own, 2), (rows, 1), 0, top)
    return jnp.take_along_axis(listing, (jnp.arange(top)[None, :] + turn) % top, axis=1)


def portions_of(count, total, reach, skew, full):
    portions = [(1 << 20) // math.isqrt(standing ** skew) + 1 for standing in range(1, count + 1)]
    largest = reach if full else min(reach, max(-(-total // count), total * portions[0] // sum(portions)))
    least = 1 if total - largest >= count - 1 else 0
    holding, spare = [largest] + [least] * (count - 1), total - largest - least * (count - 1)
    while spare > 0:
        free = [i for i in range(1, count) if holding[i] < largest] or [i for i in range(1, count) if holding[i] < reach]
        mass, budget = sum([portions[i] for i in free]), spare
        for i in free:
            more = min(reach - holding[i], max(1, budget * portions[i] // mass), spare)
            holding[i] = holding[i] + more
            spare = spare - more
    return np.array(holding)


def bell_draw(rng, extent, spread, reach, shards=(), kind=jnp.bfloat16):
    values = spread * jax.random.normal(rng, extent, jnp.float32)
    if shards:
        values = values * block_levels(rng, extent, shards, -0.22, 0.18)
    return jnp.clip(values, -reach, reach).astype(kind)


def setup_inputs(seed: int = 0) -> dict:
    key_of = jax.random.split(jax.random.key(seed), 7)
    tokens = draw_tokens(jax.random.fold_in(key_of[6], 71), 0)
    norm_gain = jnp.clip(1.0 + 0.18 * jax.random.normal(key_of[1], (D,), jnp.float32), 0.1, 1.9)
    route_expert_keys = jax.random.split(jax.random.fold_in(key_of[2], 1), TOKENS // TOK_GRP)
    route_expert_turns = jax.random.permutation(jax.random.fold_in(key_of[2], 3), TOKENS // TOK_GRP)
    route_expert = jax.vmap(lambda own, number: routed_block(jax.random.fold_in(key_of[2], 2), own, number, TOK_GRP, EXPERTS, TOPK_IN, CAP, 2))(route_expert_keys, route_expert_turns).reshape((TOKENS, TOPK_IN))
    route_gate = jnp.clip(0.29882812 + 2.2011719 * jax.random.uniform(key_of[3], (TOKENS, TOPK_IN), jnp.float32) ** block_levels(key_of[3], (TOKENS, TOPK_IN), ((0, 64),), -0.2, 0.2), 0.29882812, 2.5).astype(jnp.bfloat16)
    w_gate_up = bell_draw(key_of[4], (EXPERTS, D, 2 * FF_E), D ** -0.5, 0.0625, ((0, 64), (1, 16)))
    w_down = bell_draw(key_of[5], (EXPERTS, FF_E, D), FF_E ** -0.5, 0.1875, ((0, 64), (2, 16)))
    return {"tokens": tokens, "norm_gain": norm_gain, "route_expert": route_expert, "route_gate": route_gate, "w_gate_up": w_gate_up, "w_down": w_down}


NORM_EPS = 1e-06

def reference(tokens, norm_gain, route_expert, route_gate, w_gate_up, w_down):
    values = tokens.astype(jnp.float32)
    squares = lax.optimization_barrier(jnp.sum(values * values, axis=1, keepdims=True))
    normed = (values * lax.rsqrt(squares / D + NORM_EPS) * norm_gain[None, :].astype(jnp.float32)).astype(jnp.bfloat16)
    width = D // N_SLOT
    slots = N_GROUP * CAP
    chosen = route_expert.reshape(N_GROUP, TOK_GRP * TOPK_IN).astype(jnp.int32)
    onehot = (chosen[:, :, None] == jnp.arange(EXPERTS, dtype=jnp.int32)[None, None, :]).astype(jnp.int32)
    before = jnp.cumsum(onehot, axis=1) - onehot
    place = lax.optimization_barrier(jnp.sum(before * onehot, axis=2)).astype(jnp.int32)
    group_of = jnp.broadcast_to(jnp.arange(N_GROUP, dtype=jnp.int32)[:, None], place.shape)
    token_of = group_of * TOK_GRP + (jnp.arange(TOK_GRP * TOPK_IN, dtype=jnp.int32) // TOPK_IN)[None, :]
    table = jnp.zeros((EXPERTS, N_GROUP, CAP), jnp.int32).at[chosen, group_of, place].set(token_of)
    gains = route_gate.reshape(N_GROUP, TOK_GRP * TOPK_IN).astype(jnp.float32)
    gate_table = jnp.zeros((EXPERTS, N_GROUP, CAP), jnp.float32).at[chosen, group_of, place].set(gains)
    live = jnp.zeros((EXPERTS, N_GROUP, CAP), jnp.float32).at[chosen, group_of, place].set(1.0)

    def serve(expert, total):
        rows_at = lax.dynamic_index_in_dim(table, expert, 0, keepdims=False).reshape(slots)
        mask = lax.dynamic_index_in_dim(live, expert, 0, keepdims=False).reshape(slots)
        gate_at = lax.dynamic_index_in_dim(gate_table, expert, 0, keepdims=False).reshape(slots)
        rows = (normed[rows_at].astype(jnp.float32) * mask[:, None]).astype(jnp.bfloat16)
        w_in = lax.dynamic_index_in_dim(w_gate_up, expert, 0, keepdims=False).astype(jnp.float32)
        w_in = w_in.reshape(N_SLOT, width, 2 * FF_E)
        blocks = rows.astype(jnp.float32).reshape(slots, N_SLOT, width)
        parts = jnp.einsum('rsd,sdf->srf', blocks, w_in)
        parts = lax.optimization_barrier(parts.astype(jnp.bfloat16)).astype(jnp.float32)
        summed = lax.optimization_barrier(jnp.sum(parts, axis=0))
        hidden = (jax.nn.silu(summed[:, :FF_E]) * summed[:, FF_E:]).astype(jnp.bfloat16)
        w_out = lax.dynamic_index_in_dim(w_down, expert, 0, keepdims=False)
        result = jnp.dot(hidden, w_out, preferred_element_type=jnp.float32).astype(jnp.bfloat16)
        return total.at[rows_at].add(gate_at[:, None] * result.astype(jnp.float32))
    total = lax.fori_loop(0, EXPERTS, serve, jnp.zeros((TOKENS, D), jnp.float32))
    return total.astype(jnp.bfloat16)
```

```python
import jax
import jax.numpy as jnp
from jax import lax
from jax.sharding import PartitionSpec as P

D = 7168


NORM_EPS = 1e-06
LANES = 128


def split_rows(values):
    high = lax.reduce_precision(values, 8, 7)
    low = values - high
    column = jnp.arange(LANES, dtype=jnp.int32)[None, :]
    block = jnp.where(column == 0, high[:, None], jnp.where(column == 1, low[:, None], 0.0))
    return block.astype(jnp.bfloat16)


def expert_rows(arrived, norm_gain, w_gate_up, w_down):
    slots = arrived.shape[0]
    ways = lax.axis_size("slot")
    both = w_gate_up.shape[2]
    inner = both // 2
    every = [list(range(ways))]
    values = arrived.astype(jnp.float32)
    squares = jnp.sum(values * values, axis=1)
    gained = (values * norm_gain[None, :]).astype(jnp.bfloat16)
    partial = jnp.dot(gained, w_gate_up[0], preferred_element_type=jnp.float32).astype(jnp.bfloat16)
    sent = jnp.concatenate([partial, split_rows(squares)], axis=1)
    pieces = lax.all_to_all(
        sent.reshape(ways, slots // ways, both + LANES),
        "slot",
        split_axis=0,
        concat_axis=0,
        tiled=True,
        axis_index_groups=every,
    )
    mine = jnp.sum(pieces.astype(jnp.float32), axis=0)
    scale = lax.rsqrt((mine[:, both : both + 1] + mine[:, both + 1 : both + 2]) / D + NORM_EPS)
    gate, up = mine[:, :inner] * scale, mine[:, inner:both] * scale
    hidden = (jax.nn.silu(gate) * up).astype(jnp.bfloat16)
    spread = lax.all_to_all(
        jnp.broadcast_to(hidden[None], (ways,) + hidden.shape),
        "slot",
        split_axis=0,
        concat_axis=0,
        tiled=True,
        axis_index_groups=every,
    )
    result = jnp.dot(spread.reshape(slots, inner), w_down[0], preferred_element_type=jnp.float32)
    return result.astype(jnp.bfloat16)


def local(tokens, norm_gain, route_expert, route_gate, w_gate_up, w_down):
    tok_rows, width = tokens.shape
    groups = lax.axis_size("group")
    picks = route_expert.shape[1]
    capacity = 2 * tok_rows * picks // groups
    slots = groups * capacity
    flat_routes = route_expert.reshape(-1)
    chosen = (flat_routes[:, None] == jnp.arange(groups, dtype=jnp.int32)[None, :]).astype(
        jnp.int32
    )
    before = jnp.cumsum(chosen, axis=0) - chosen
    place = jnp.sum(before * chosen, axis=1)
    target = flat_routes * capacity + place
    picked = (target[:, None] == jnp.arange(slots, dtype=jnp.int32)[None, :]).reshape(
        tok_rows, picks, slots
    )
    spread = jnp.sum(picked.astype(jnp.float32), axis=1).astype(jnp.bfloat16)
    weights_back = jnp.sum(
        picked.astype(jnp.float32) * route_gate.astype(jnp.float32)[:, :, None], axis=1
    ).astype(jnp.bfloat16)
    outgoing = jnp.einsum("tr,td->rd", spread, tokens, preferred_element_type=jnp.float32)
    outgoing = outgoing.astype(jnp.bfloat16).reshape(groups, capacity, width)
    arrived = lax.all_to_all(outgoing, "group", split_axis=0, concat_axis=0, tiled=True)
    finished = expert_rows(
        arrived.reshape(slots, width), norm_gain, w_gate_up, w_down
    ).reshape(groups, capacity, width)
    returned = lax.all_to_all(finished, "group", split_axis=0, concat_axis=0, tiled=True)
    mixed = jnp.dot(
        weights_back, returned.reshape(slots, width), preferred_element_type=jnp.float32
    )
    return mixed.astype(jnp.bfloat16)


def solution(mesh):
    placed = (
        P("group", "slot"),
        P("slot"),
        P("group", None),
        P("group", None),
        P("group", "slot", None),
        P("group", None, "slot"),
    )
    return jax.shard_map(
        local, mesh=mesh, in_specs=placed, out_specs=P("group", "slot"), check_vma=False
    )
```

```python
import functools

import jax
import jax.numpy as jnp
from jax import lax
from jax.experimental import pallas as pl
from jax.experimental.pallas import tpu as pltpu
from jax.sharding import PartitionSpec as P

D = 7168


NORM_EPS = 1e-06
LANES = 128
CORES = 2


def place_rows(experts, capacity, routes_ref, tokens_ref, rows_ref, target_ref):
    slots = rows_ref.shape[0]
    count = tokens_ref.shape[1]
    first, second = routes_ref[0:1, :], routes_ref[1:2, :]
    names = lax.broadcasted_iota(jnp.int32, (experts, count), 0)
    one = (names == first).astype(jnp.float32)
    two = (names == second).astype(jnp.float32)
    earlier = lax.broadcasted_iota(jnp.int32, (count, count), 0) < lax.broadcasted_iota(
        jnp.int32, (count, count), 1
    )
    before = jnp.dot(
        (one + two).astype(jnp.bfloat16),
        earlier.astype(jnp.float32).astype(jnp.bfloat16),
        preferred_element_type=jnp.float32,
    )
    place_one = jnp.sum(one * before, axis=0, keepdims=True).astype(jnp.int32)
    place_two = jnp.sum(two * (before + one), axis=0, keepdims=True).astype(jnp.int32)
    slot_one, slot_two = first * capacity + place_one, second * capacity + place_two
    target_ref[0:1, :] = slot_one
    target_ref[1:2, :] = slot_two
    row = lax.broadcasted_iota(jnp.int32, (slots, count), 0)
    picked = jnp.where((row == slot_one) | (row == slot_two), 1.0, 0.0).astype(jnp.bfloat16)
    rows_ref[...] = lax.dot_general(
        picked, tokens_ref[...], (((1,), (1,)), ((), ())), preferred_element_type=jnp.float32
    ).astype(jnp.bfloat16)


def split_rows(values):
    high = lax.reduce_precision(values, 8, 7)
    low = values - high
    column = jnp.arange(LANES, dtype=jnp.int32)[None, :]
    block = jnp.where(column == 0, high[:, None], jnp.where(column == 1, low[:, None], 0.0))
    return block.astype(jnp.bfloat16)


def partial_rows(arrived, norm_gain, w_gate_up):
    values = arrived.astype(jnp.float32)
    squares = jnp.sum(values * values, axis=1)
    gained = (values * norm_gain[None, :]).astype(jnp.bfloat16)
    partial = jnp.dot(gained, w_gate_up, preferred_element_type=jnp.float32).astype(jnp.bfloat16)
    return jnp.concatenate([partial, split_rows(squares)], axis=1)


def exchange(values, axis, members):
    return lax.all_to_all(
        values, axis, split_axis=0, concat_axis=0, tiled=True, axis_index_groups=members
    )


def local(tokens, norm_gain, route_expert, route_gate, w_gate_up, w_down):
    tok_rows, width = tokens.shape
    groups = lax.axis_size("group")
    ways = lax.axis_size("slot")
    chips = groups // CORES
    picks = route_expert.shape[1]
    capacity = 2 * tok_rows * picks // groups
    slots = groups * capacity
    half = chips * capacity
    both = w_gate_up.shape[2]
    inner = both // 2
    columns = [[CORES * chip + core for chip in range(chips)] for core in range(CORES)]
    swap = [(index, index ^ 1) for index in range(groups)]
    every = [list(range(ways))]

    routes = route_expert.T ^ (lax.axis_index("group") % CORES)
    rows, target = pl.pallas_call(
        functools.partial(place_rows, groups, capacity),
        out_shape=(
            jax.ShapeDtypeStruct((slots, width), jnp.bfloat16),
            jax.ShapeDtypeStruct((picks, tok_rows), jnp.int32),
        ),
        name="place_rows",
    )(routes, tokens.T)
    gates = route_gate.T
    row = lax.broadcasted_iota(jnp.int32, (slots, tok_rows), 0)
    weights_back = jnp.where(row == target[0:1], gates[0:1], 0) + jnp.where(
        row == target[1:2], gates[1:2], 0
    )

    arrived = exchange(rows.reshape(chips, CORES * capacity, width), "group", columns)
    other_gate_up = lax.ppermute(w_gate_up, "group", swap)
    other_down = lax.ppermute(w_down, "group", swap)
    arrived = arrived.reshape(chips, CORES, capacity, width)
    sent = jnp.concatenate(
        [
            partial_rows(arrived[:, 0].reshape(half, width), norm_gain, w_gate_up[0]),
            partial_rows(arrived[:, 1].reshape(half, width), norm_gain, other_gate_up[0]),
        ],
        axis=0,
    )
    pieces = exchange(sent.reshape(ways, slots // ways, both + LANES), "slot", every)
    mine = jnp.sum(pieces.astype(jnp.float32), axis=0)
    scale = lax.rsqrt((mine[:, both : both + 1] + mine[:, both + 1 : both + 2]) / D + NORM_EPS)
    gate, up = mine[:, :inner] * scale, mine[:, inner:both] * scale
    hidden = (jax.nn.silu(gate) * up).astype(jnp.bfloat16)
    spread = exchange(jnp.broadcast_to(hidden[None], (ways,) + hidden.shape), "slot", every)
    spread = spread.reshape(slots, inner)
    finished = jnp.concatenate(
        [
            jnp.dot(spread[:half], w_down[0], preferred_element_type=jnp.float32)
            .astype(jnp.bfloat16)
            .reshape(chips, capacity, width),
            jnp.dot(spread[half:], other_down[0], preferred_element_type=jnp.float32)
            .astype(jnp.bfloat16)
            .reshape(chips, capacity, width),
        ],
        axis=1,
    )
    returned = exchange(finished, "group", columns).reshape(slots, width)
    mixed = lax.dot_general(
        returned, weights_back, (((0,), (0,)), ((), ())), preferred_element_type=jnp.float32
    )
    return mixed.astype(jnp.bfloat16).T


def solution(mesh):
    placed = (
        P("group", "slot"),
        P("slot"),
        P("group", None),
        P("group", None),
        P("group", "slot", None),
        P("group", None, "slot"),
    )
    return jax.shard_map(
        local, mesh=mesh, in_specs=placed, out_specs=P("group", "slot"), check_vma=False
    )
```

```python
import functools

import jax
import jax.numpy as jnp
from jax import lax
from jax.experimental import pallas as pl
from jax.experimental.pallas import tpu as pltpu
from jax.sharding import PartitionSpec as P

D = 7168


NORM_EPS = 1e-06
LANES = 128
STRIP = 512
VMEM_BYTES = 32 * 1024 * 1024
CORES = 2


def place_rows(experts, capacity, routes_ref, tokens_ref, rows_ref, target_ref):
    slots = rows_ref.shape[0]
    count = tokens_ref.shape[1]
    core = lax.rem(lax.axis_index("group"), CORES)
    first, second = routes_ref[0:1, :] ^ core, routes_ref[1:2, :] ^ core
    names = lax.broadcasted_iota(jnp.int32, (experts, count), 0)
    one = (names == first).astype(jnp.float32)
    two = (names == second).astype(jnp.float32)
    earlier = lax.broadcasted_iota(jnp.int32, (count, count), 0) < lax.broadcasted_iota(
        jnp.int32, (count, count), 1
    )
    before = jnp.dot(
        (one + two).astype(jnp.bfloat16),
        earlier.astype(jnp.float32).astype(jnp.bfloat16),
        preferred_element_type=jnp.float32,
    )
    place_one = jnp.sum(one * before, axis=0, keepdims=True).astype(jnp.int32)
    place_two = jnp.sum(two * (before + one), axis=0, keepdims=True).astype(jnp.int32)
    slot_one, slot_two = first * capacity + place_one, second * capacity + place_two
    target_ref[0:1, :] = slot_one
    target_ref[1:2, :] = slot_two
    row = lax.broadcasted_iota(jnp.int32, (slots, count), 0)
    picked = jnp.where((row == slot_one) | (row == slot_two), 1.0, 0.0).astype(jnp.bfloat16)
    rows_ref[...] = lax.dot_general(
        picked, tokens_ref[...], (((1,), (1,)), ((), ())), preferred_element_type=jnp.float32
    ).astype(jnp.bfloat16)


def partial_rows(arrived_ref, gain_ref, near_ref, far_ref, sent_ref):
    half = sent_ref.shape[0] // CORES
    both = far_ref.shape[1]
    values = arrived_ref[...].astype(jnp.float32)
    capacity = values.shape[1] // CORES
    column = lax.broadcasted_iota(jnp.int32, (half, LANES), 1)
    for which, weights in enumerate((near_ref, far_ref)):
        mine = values[:, which * capacity : (which + 1) * capacity].reshape(half, -1)
        squares = jnp.sum(mine * mine, axis=1, keepdims=True)
        high = squares.astype(jnp.bfloat16).astype(jnp.float32)
        gained = (mine * gain_ref[0:1, :]).astype(jnp.bfloat16)
        rows = slice(which * half, (which + 1) * half)
        sent_ref[rows, both:] = jnp.where(
            column == 0, high, jnp.where(column == 1, squares - high, 0.0)
        ).astype(jnp.bfloat16)
        for start in range(0, both, STRIP):
            sent_ref[rows, start : start + STRIP] = jnp.dot(
                gained, weights[:, start : start + STRIP], preferred_element_type=jnp.float32
            ).astype(jnp.bfloat16)


def down_rows(hidden_ref, near_ref, far_ref, finished_ref):
    half = hidden_ref.shape[0] // CORES
    chips, capacity, width = finished_ref.shape
    results = [
        lax.dot_general(
            hidden_ref[which * half : (which + 1) * half, :],
            weights[...],
            (((1,), (1,)), ((), ())),
            preferred_element_type=jnp.float32,
        ).reshape(chips, capacity // CORES, width)
        for which, weights in enumerate((near_ref, far_ref))
    ]
    finished_ref[...] = jnp.concatenate(results, axis=1).astype(jnp.bfloat16)


def exchange(values, axis, members):
    return lax.all_to_all(
        values, axis, split_axis=0, concat_axis=0, tiled=True, axis_index_groups=members
    )


def local(tokens, norm_gain, route_expert, route_gate, w_gate_up, w_down):
    tok_rows, width = tokens.shape
    groups = lax.axis_size("group")
    ways = lax.axis_size("slot")
    chips = groups // CORES
    picks = route_expert.shape[1]
    capacity = 2 * tok_rows * picks // groups
    slots = groups * capacity
    both = w_gate_up.shape[2]
    inner = both // 2
    columns = [[CORES * chip + core for chip in range(chips)] for core in range(CORES)]
    swap = [(index, index ^ 1) for index in range(groups)]
    every = [list(range(ways))]

    rows, target = pl.pallas_call(
        functools.partial(place_rows, groups, capacity),
        out_shape=(
            jax.ShapeDtypeStruct((slots, width), jnp.bfloat16),
            jax.ShapeDtypeStruct((picks, tok_rows), jnp.int32),
        ),
        name="place_rows",
    )(route_expert.T, tokens.T)
    gates = route_gate.T
    row = lax.broadcasted_iota(jnp.int32, (slots, tok_rows), 0)
    weights_back = jnp.where(row == target[0:1], gates[0:1], 0) + jnp.where(
        row == target[1:2], gates[1:2], 0
    )

    arrived = exchange(rows.reshape(chips, CORES * capacity, width), "group", columns)
    other_gate_up = lax.ppermute(w_gate_up, "group", swap)
    other_down = lax.ppermute(w_down, "group", swap)
    whole = pl.BlockSpec(memory_space=pltpu.VMEM)
    gain = jnp.broadcast_to(norm_gain[None], (8, width))
    arrived, gain, other_gate_up, other_down, weights_back = lax.optimization_barrier(
        (arrived, gain, other_gate_up, other_down, weights_back)
    )
    sent = pl.pallas_call(
        partial_rows,
        out_shape=jax.ShapeDtypeStruct((slots, both + LANES), jnp.bfloat16),
        in_specs=[whole] * 4,
        out_specs=whole,
        compiler_params=pltpu.CompilerParams(vmem_limit_bytes=VMEM_BYTES),
        cost_estimate=pl.CostEstimate(
            flops=2 * slots * width * both, bytes_accessed=8 * width * both, transcendentals=0
        ),
        name="partial_rows",
    )(arrived, gain, w_gate_up[0], other_gate_up[0])
    pieces = exchange(sent.reshape(ways, slots // ways, both + LANES), "slot", every)
    mine = jnp.sum(pieces.astype(jnp.float32), axis=0)
    scale = lax.rsqrt((mine[:, both : both + 1] + mine[:, both + 1 : both + 2]) / D + NORM_EPS)
    gate, up = mine[:, :inner] * scale, mine[:, inner:both] * scale
    hidden = (jax.nn.silu(gate) * up).astype(jnp.bfloat16)
    spread = exchange(jnp.broadcast_to(hidden[None], (ways,) + hidden.shape), "slot", every)
    finished = pl.pallas_call(
        down_rows,
        out_shape=jax.ShapeDtypeStruct((chips, CORES * capacity, width), jnp.bfloat16),
        in_specs=[whole] * 3,
        out_specs=whole,
        compiler_params=pltpu.CompilerParams(vmem_limit_bytes=VMEM_BYTES),
        cost_estimate=pl.CostEstimate(
            flops=2 * slots * width * inner, bytes_accessed=6 * width * inner, transcendentals=0
        ),
        name="down_rows",
    )(spread.reshape(slots, inner), w_down[0].T, other_down[0].T)
    returned = exchange(finished, "group", columns).reshape(slots, width)
    mixed = lax.dot_general(
        returned, weights_back, (((0,), (0,)), ((), ())), preferred_element_type=jnp.float32
    )
    return mixed.astype(jnp.bfloat16).T


def solution(mesh):
    placed = (
        P("group", "slot"),
        P("slot"),
        P("group", None),
        P("group", None),
        P("group", "slot", None),
        P("group", None, "slot"),
    )
    return jax.shard_map(
        local, mesh=mesh, in_specs=placed, out_specs=P("group", "slot"), check_vma=False
    )
```

```python
import functools

import jax
import jax.numpy as jnp
from jax import lax
from jax.experimental import pallas as pl
from jax.experimental.pallas import tpu as pltpu
from jax.sharding import PartitionSpec as P

D = 7168


NORM_EPS = 1e-06
LANES = 128
STRIP = 512
VMEM_BYTES = 32 * 1024 * 1024
CORES = 2


def place_rows(experts, capacity, routes_ref, tokens_ref, rows_ref, target_ref):
    slots = rows_ref.shape[0]
    count = tokens_ref.shape[1]
    core = lax.rem(lax.axis_index("group"), CORES)
    first, second = routes_ref[0:1, :] ^ core, routes_ref[1:2, :] ^ core
    names = lax.broadcasted_iota(jnp.int32, (experts, count), 0)
    one = (names == first).astype(jnp.float32)
    two = (names == second).astype(jnp.float32)
    earlier = lax.broadcasted_iota(jnp.int32, (count, count), 0) < lax.broadcasted_iota(
        jnp.int32, (count, count), 1
    )
    before = jnp.dot(
        (one + two).astype(jnp.bfloat16),
        earlier.astype(jnp.float32).astype(jnp.bfloat16),
        preferred_element_type=jnp.float32,
    )
    place_one = jnp.sum(one * before, axis=0, keepdims=True).astype(jnp.int32)
    place_two = jnp.sum(two * (before + one), axis=0, keepdims=True).astype(jnp.int32)
    slot_one, slot_two = first * capacity + place_one, second * capacity + place_two
    target_ref[0:1, :] = slot_one
    target_ref[1:2, :] = slot_two
    row = lax.broadcasted_iota(jnp.int32, (slots, count), 0)
    picked = jnp.where((row == slot_one) | (row == slot_two), 1.0, 0.0).astype(jnp.bfloat16)
    rows_ref[...] = lax.dot_general(
        picked, tokens_ref[...], (((1,), (1,)), ((), ())), preferred_element_type=jnp.float32
    ).astype(jnp.bfloat16)


def partial_rows(which, arrived_ref, *refs):
    weights, sent_ref = refs[:-1], refs[-1]
    half, columns = sent_ref.shape
    both = columns - LANES
    values = arrived_ref[...].astype(jnp.float32)
    capacity = values.shape[1] // CORES
    column = lax.broadcasted_iota(jnp.int32, (half, LANES), 1)
    mine = values[:, which * capacity : (which + 1) * capacity].reshape(half, -1)
    exact = mine.astype(jnp.bfloat16)
    squares = jnp.sum(mine * mine, axis=1, keepdims=True)
    high = squares.astype(jnp.bfloat16).astype(jnp.float32)
    sent_ref[:, both:] = jnp.where(
        column == 0, high, jnp.where(column == 1, squares - high, 0.0)
    ).astype(jnp.bfloat16)
    done = 0
    for part in weights:
        for start in range(0, part.shape[1], STRIP):
            sent_ref[:, done : done + STRIP] = jnp.dot(
                exact, part[:, start : start + STRIP], preferred_element_type=jnp.float32
            ).astype(jnp.bfloat16)
            done += STRIP


def down_rows(hidden_ref, near_ref, far_ref, finished_ref):
    half = hidden_ref.shape[0] // CORES
    chips, capacity, width = finished_ref.shape
    results = [
        lax.dot_general(
            hidden_ref[which * half : (which + 1) * half, :],
            weights[...],
            (((1,), (1,)), ((), ())),
            preferred_element_type=jnp.float32,
        ).reshape(chips, capacity // CORES, width)
        for which, weights in enumerate((near_ref, far_ref))
    ]
    finished_ref[...] = jnp.concatenate(results, axis=1).astype(jnp.bfloat16)


def exchange(values, axis, members):
    return lax.all_to_all(
        values, axis, split_axis=0, concat_axis=0, tiled=True, axis_index_groups=members
    )


def local(tokens, norm_gain, route_expert, route_gate, w_gate_up, w_down):
    tok_rows, width = tokens.shape
    groups = lax.axis_size("group")
    ways = lax.axis_size("slot")
    chips = groups // CORES
    picks = route_expert.shape[1]
    capacity = 2 * tok_rows * picks // groups
    slots = groups * capacity
    both = w_gate_up.shape[2]
    inner = both // 2
    columns = [[CORES * chip + core for chip in range(chips)] for core in range(CORES)]
    swap = [(index, index ^ 1) for index in range(groups)]
    every = [list(range(ways))]

    rows, target = pl.pallas_call(
        functools.partial(place_rows, groups, capacity),
        out_shape=(
            jax.ShapeDtypeStruct((slots, width), jnp.bfloat16),
            jax.ShapeDtypeStruct((picks, tok_rows), jnp.int32),
        ),
        name="place_rows",
    )(route_expert.T, tokens.T)
    gates = route_gate.T
    row = lax.broadcasted_iota(jnp.int32, (slots, tok_rows), 0)
    weights_back = jnp.where(row == target[0:1], gates[0:1], 0) + jnp.where(
        row == target[1:2], gates[1:2], 0
    )

    arrived = exchange(rows.reshape(chips, CORES * capacity, width), "group", columns)
    gained = (w_gate_up[0].astype(jnp.float32) * norm_gain[:, None]).astype(jnp.bfloat16)
    other_gate = lax.ppermute(gained[:, :inner], "group", swap)
    other_up = lax.ppermute(gained[:, inner:], "group", swap)
    other_down = lax.ppermute(w_down, "group", swap)
    whole = pl.BlockSpec(memory_space=pltpu.VMEM)
    arrived, gained, other_gate, other_up, other_down, weights_back = lax.optimization_barrier(
        (arrived, gained, other_gate, other_up, other_down, weights_back)
    )

    def products(which, *weights):
        return pl.pallas_call(
            functools.partial(partial_rows, which),
            out_shape=jax.ShapeDtypeStruct((slots // CORES, both + LANES), jnp.bfloat16),
            in_specs=[whole] * (1 + len(weights)),
            out_specs=whole,
            compiler_params=pltpu.CompilerParams(vmem_limit_bytes=VMEM_BYTES),
            cost_estimate=pl.CostEstimate(
                flops=slots * width * both, bytes_accessed=4 * width * both, transcendentals=0
            ),
            name="partial_rows",
        )(arrived, *weights)

    sent = jnp.concatenate(
        [products(0, gained), products(1, other_gate, other_up)], axis=0
    )
    pieces = exchange(sent.reshape(ways, slots // ways, both + LANES), "slot", every)
    mine = jnp.sum(pieces.astype(jnp.float32), axis=0)
    scale = lax.rsqrt((mine[:, both : both + 1] + mine[:, both + 1 : both + 2]) / D + NORM_EPS)
    gate, up = mine[:, :inner] * scale, mine[:, inner:both] * scale
    hidden = (jax.nn.silu(gate) * up).astype(jnp.bfloat16)
    spread = exchange(jnp.broadcast_to(hidden[None], (ways,) + hidden.shape), "slot", every)
    finished = pl.pallas_call(
        down_rows,
        out_shape=jax.ShapeDtypeStruct((chips, CORES * capacity, width), jnp.bfloat16),
        in_specs=[whole] * 3,
        out_specs=whole,
        compiler_params=pltpu.CompilerParams(vmem_limit_bytes=VMEM_BYTES),
        cost_estimate=pl.CostEstimate(
            flops=2 * slots * width * inner, bytes_accessed=6 * width * inner, transcendentals=0
        ),
        name="down_rows",
    )(spread.reshape(slots, inner), w_down[0].T, other_down[0].T)
    returned = exchange(finished, "group", columns).reshape(slots, width)
    mixed = lax.dot_general(
        returned, weights_back, (((0,), (0,)), ((), ())), preferred_element_type=jnp.float32
    )
    return mixed.astype(jnp.bfloat16).T


def solution(mesh):
    placed = (
        P("group", "slot"),
        P("slot"),
        P("group", None),
        P("group", None),
        P("group", "slot", None),
        P("group", None, "slot"),
    )
    return jax.shard_map(
        local, mesh=mesh, in_specs=placed, out_specs=P("group", "slot"), check_vma=False
    )
```

```python
import functools
import math

import jax
import jax.numpy as jnp
from jax import lax
from jax.experimental import pallas as pl
from jax.experimental.pallas import tpu as pltpu
from jax.sharding import PartitionSpec as P

D = 7168


NORM_EPS = 1e-06
LANES = 128
STRIP = 512
VMEM_BYTES = 32 * 1024 * 1024
CORES = 2


def place_rows(experts, capacity, routes_ref, tokens_ref, rows_ref, target_ref):
    slots = rows_ref.shape[0]
    count = tokens_ref.shape[1]
    core = lax.rem(lax.axis_index("group"), CORES)
    first, second = routes_ref[0:1, :] ^ core, routes_ref[1:2, :] ^ core
    names = lax.broadcasted_iota(jnp.int32, (experts, count), 0)
    one = (names == first).astype(jnp.float32)
    two = (names == second).astype(jnp.float32)
    earlier = lax.broadcasted_iota(jnp.int32, (count, count), 0) < lax.broadcasted_iota(
        jnp.int32, (count, count), 1
    )
    before = jnp.dot(
        (one + two).astype(jnp.bfloat16),
        earlier.astype(jnp.float32).astype(jnp.bfloat16),
        preferred_element_type=jnp.float32,
    )
    place_one = jnp.sum(one * before, axis=0, keepdims=True).astype(jnp.int32)
    place_two = jnp.sum(two * (before + one), axis=0, keepdims=True).astype(jnp.int32)
    slot_one, slot_two = first * capacity + place_one, second * capacity + place_two
    target_ref[0:1, :] = slot_one
    target_ref[1:2, :] = slot_two
    row = lax.broadcasted_iota(jnp.int32, (slots, count), 0)
    picked = jnp.where((row == slot_one) | (row == slot_two), 1.0, 0.0).astype(jnp.bfloat16)
    rows_ref[...] = lax.dot_general(
        picked, tokens_ref[...], (((1,), (1,)), ((), ())), preferred_element_type=jnp.float32
    ).astype(jnp.bfloat16)


def partial_rows(which, arrived_ref, *refs):
    weights, sent_ref = refs[:-1], refs[-1]
    half, columns = sent_ref.shape
    both = columns - LANES
    values = arrived_ref[...].astype(jnp.float32)
    capacity = values.shape[1] // CORES
    column = lax.broadcasted_iota(jnp.int32, (half, LANES), 1)
    mine = values[:, which * capacity : (which + 1) * capacity].reshape(half, -1)
    exact = mine.astype(jnp.bfloat16)
    squares = jnp.sum(mine * mine, axis=1, keepdims=True)
    high = squares.astype(jnp.bfloat16).astype(jnp.float32)
    sent_ref[:, both:] = jnp.where(
        column == 0, high, jnp.where(column == 1, squares - high, 0.0)
    ).astype(jnp.bfloat16)
    done = 0
    for part in weights:
        for start in range(0, part.shape[1], STRIP):
            sent_ref[:, done : done + STRIP] = jnp.dot(
                exact, part[:, start : start + STRIP], preferred_element_type=jnp.float32
            ).astype(jnp.bfloat16)
            done += STRIP


def merge_rows(pieces_ref, merged_ref):
    rows, columns = merged_ref.shape
    both = columns - LANES
    for start in range(0, both, STRIP):
        strip = slice(start, start + STRIP)
        merged_ref[:, strip] = jnp.sum(pieces_ref[:, :, strip].astype(jnp.float32), axis=0).astype(
            jnp.bfloat16
        )
    tail = jnp.sum(pieces_ref[:, :, both:].astype(jnp.float32), axis=0)
    squares = tail[:, 0:1] + tail[:, 1:2]
    high = squares.astype(jnp.bfloat16).astype(jnp.float32)
    column = lax.broadcasted_iota(jnp.int32, (rows, LANES), 1)
    merged_ref[:, both:] = jnp.where(
        column == 0, high, jnp.where(column == 1, squares - high, 0.0)
    ).astype(jnp.bfloat16)


def down_rows(hidden_ref, near_ref, far_ref, finished_ref):
    half = hidden_ref.shape[0] // CORES
    chips, capacity, width = finished_ref.shape
    results = [
        lax.dot_general(
            hidden_ref[which * half : (which + 1) * half, :],
            weights[...],
            (((1,), (1,)), ((), ())),
            preferred_element_type=jnp.float32,
        ).reshape(chips, capacity // CORES, width)
        for which, weights in enumerate((near_ref, far_ref))
    ]
    finished_ref[...] = jnp.concatenate(results, axis=1).astype(jnp.bfloat16)


def exchange(values, axis, members):
    return lax.all_to_all(
        values, axis, split_axis=0, concat_axis=0, tiled=True, axis_index_groups=members
    )


def local(tokens, norm_gain, route_expert, route_gate, w_gate_up, w_down):
    tok_rows, width = tokens.shape
    groups = lax.axis_size("group")
    ways = lax.axis_size("slot")
    chips = groups // CORES
    picks = route_expert.shape[1]
    capacity = 2 * tok_rows * picks // groups
    slots = groups * capacity
    both = w_gate_up.shape[2]
    inner = both // 2
    columns = [[CORES * chip + core for chip in range(chips)] for core in range(CORES)]
    swap = [(index, index ^ 1) for index in range(groups)]
    side = math.isqrt(ways)
    places = [
        [
            [group * ways + (side * b + a if group % CORES == 0 else side * a + b) for b in range(side)]
            for a in range(side)
        ]
        for group in range(groups)
    ]
    first_lines = [[line[b] for line in part] for part in places for b in range(side)]
    second_lines = [line for part in places for line in part]
    planes = [[place for line in part for place in line] for part in places]
    everywhere = ("group", "slot")

    rows, target = pl.pallas_call(
        functools.partial(place_rows, groups, capacity),
        out_shape=(
            jax.ShapeDtypeStruct((slots, width), jnp.bfloat16),
            jax.ShapeDtypeStruct((picks, tok_rows), jnp.int32),
        ),
        name="place_rows",
    )(route_expert.T, tokens.T)
    gates = route_gate.T
    row = lax.broadcasted_iota(jnp.int32, (slots, tok_rows), 0)
    weights_back = jnp.where(row == target[0:1], gates[0:1], 0) + jnp.where(
        row == target[1:2], gates[1:2], 0
    )

    arrived = exchange(rows.reshape(chips, CORES * capacity, width), "group", columns)
    gained = (w_gate_up[0].astype(jnp.float32) * norm_gain[:, None]).astype(jnp.bfloat16)
    other_gate = lax.ppermute(gained[:, :inner], "group", swap)
    other_up = lax.ppermute(gained[:, inner:], "group", swap)
    other_down = lax.ppermute(w_down, "group", swap)
    whole = pl.BlockSpec(memory_space=pltpu.VMEM)
    arrived, gained, other_gate, other_up, other_down, weights_back = lax.optimization_barrier(
        (arrived, gained, other_gate, other_up, other_down, weights_back)
    )

    def products(which, *weights):
        return pl.pallas_call(
            functools.partial(partial_rows, which),
            out_shape=jax.ShapeDtypeStruct((slots // CORES, both + LANES), jnp.bfloat16),
            in_specs=[whole] * (1 + len(weights)),
            out_specs=whole,
            compiler_params=pltpu.CompilerParams(vmem_limit_bytes=VMEM_BYTES),
            cost_estimate=pl.CostEstimate(
                flops=slots * width * both, bytes_accessed=4 * width * both, transcendentals=0
            ),
            name="partial_rows",
        )(arrived, *weights)

    sent = jnp.concatenate(
        [products(0, gained), products(1, other_gate, other_up)], axis=0
    )
    pieces = exchange(sent.reshape(side, slots // side, both + LANES), everywhere, first_lines)
    merged = pl.pallas_call(
        merge_rows,
        out_shape=jax.ShapeDtypeStruct((slots // side, both + LANES), jnp.bfloat16),
        in_specs=[whole],
        out_specs=whole,
        compiler_params=pltpu.CompilerParams(vmem_limit_bytes=VMEM_BYTES),
        name="merge_rows",
    )(pieces)
    pieces = exchange(merged.reshape(side, slots // ways, both + LANES), everywhere, second_lines)
    mine = jnp.sum(pieces.astype(jnp.float32), axis=0)
    scale = lax.rsqrt((mine[:, both : both + 1] + mine[:, both + 1 : both + 2]) / D + NORM_EPS)
    gate, up = mine[:, :inner] * scale, mine[:, inner:both] * scale
    hidden = (jax.nn.silu(gate) * up).astype(jnp.bfloat16)
    spread = exchange(jnp.broadcast_to(hidden[None], (ways,) + hidden.shape), everywhere, planes)
    finished = pl.pallas_call(
        down_rows,
        out_shape=jax.ShapeDtypeStruct((chips, CORES * capacity, width), jnp.bfloat16),
        in_specs=[whole] * 3,
        out_specs=whole,
        compiler_params=pltpu.CompilerParams(vmem_limit_bytes=VMEM_BYTES),
        cost_estimate=pl.CostEstimate(
            flops=2 * slots * width * inner, bytes_accessed=6 * width * inner, transcendentals=0
        ),
        name="down_rows",
    )(spread.reshape(slots, inner), w_down[0].T, other_down[0].T)
    returned = exchange(finished, "group", columns).reshape(slots, width)
    mixed = lax.dot_general(
        returned, weights_back, (((0,), (0,)), ((), ())), preferred_element_type=jnp.float32
    )
    return mixed.astype(jnp.bfloat16).T


def solution(mesh):
    placed = (
        P("group", "slot"),
        P("slot"),
        P("group", None),
        P("group", None),
        P("group", "slot", None),
        P("group", None, "slot"),
    )
    return jax.shard_map(
        local, mesh=mesh, in_specs=placed, out_specs=P("group", "slot"), check_vma=False
    )
```

```python
import functools
import math

import jax
import jax.numpy as jnp
from jax import lax
from jax.experimental import pallas as pl
from jax.experimental.pallas import tpu as pltpu
from jax.sharding import PartitionSpec as P

D = 7168


NORM_EPS = 1e-06
LANES = 128
STRIP = 512
VMEM_BYTES = 32 * 1024 * 1024
CORES = 2


def place_rows(experts, capacity, routes_ref, tokens_ref, rows_ref, target_ref):
    slots = rows_ref.shape[0]
    count = tokens_ref.shape[1]
    core = lax.rem(lax.axis_index("group"), CORES)
    first = jnp.where(core == 0, routes_ref[0:1, :], experts - 1 - routes_ref[0:1, :])
    second = jnp.where(core == 0, routes_ref[1:2, :], experts - 1 - routes_ref[1:2, :])
    names = lax.broadcasted_iota(jnp.int32, (experts, count), 0)
    one = (names == first).astype(jnp.float32)
    two = (names == second).astype(jnp.float32)
    earlier = lax.broadcasted_iota(jnp.int32, (count, count), 0) < lax.broadcasted_iota(
        jnp.int32, (count, count), 1
    )
    before = jnp.dot(
        (one + two).astype(jnp.bfloat16),
        earlier.astype(jnp.float32).astype(jnp.bfloat16),
        preferred_element_type=jnp.float32,
    )
    place_one = jnp.sum(one * before, axis=0, keepdims=True).astype(jnp.int32)
    place_two = jnp.sum(two * (before + one), axis=0, keepdims=True).astype(jnp.int32)
    slot_one, slot_two = first * capacity + place_one, second * capacity + place_two
    target_ref[0:1, :] = slot_one
    target_ref[1:2, :] = slot_two
    row = lax.broadcasted_iota(jnp.int32, (slots, count), 0)
    picked = jnp.where((row == slot_one) | (row == slot_two), 1.0, 0.0).astype(jnp.bfloat16)
    rows_ref[...] = lax.dot_general(
        picked, tokens_ref[...], (((1,), (1,)), ((), ())), preferred_element_type=jnp.float32
    ).astype(jnp.bfloat16)


def partial_rows(which, arrived_ref, *refs):
    weights, sent_ref = refs[:-1], refs[-1]
    half, columns = sent_ref.shape
    both = columns - LANES
    values = arrived_ref[...].astype(jnp.float32)
    capacity = values.shape[1] // CORES
    column = lax.broadcasted_iota(jnp.int32, (half, LANES), 1)
    mine = values[:, which * capacity : (which + 1) * capacity].reshape(half, -1)
    exact = mine.astype(jnp.bfloat16)
    squares = jnp.sum(mine * mine, axis=1, keepdims=True)
    high = squares.astype(jnp.bfloat16).astype(jnp.float32)
    sent_ref[:, both:] = jnp.where(
        column == 0, high, jnp.where(column == 1, squares - high, 0.0)
    ).astype(jnp.bfloat16)
    done = 0
    for part in weights:
        for start in range(0, part.shape[1], STRIP):
            sent_ref[:, done : done + STRIP] = jnp.dot(
                exact, part[:, start : start + STRIP], preferred_element_type=jnp.float32
            ).astype(jnp.bfloat16)
            done += STRIP


def merge_rows(pieces_ref, merged_ref):
    rows, columns = merged_ref.shape
    both = columns - LANES
    for start in range(0, both, STRIP):
        strip = slice(start, start + STRIP)
        merged_ref[:, strip] = jnp.sum(pieces_ref[:, :, strip].astype(jnp.float32), axis=0).astype(
            jnp.bfloat16
        )
    tail = jnp.sum(pieces_ref[:, :, both:].astype(jnp.float32), axis=0)
    squares = tail[:, 0:1] + tail[:, 1:2]
    high = squares.astype(jnp.bfloat16).astype(jnp.float32)
    column = lax.broadcasted_iota(jnp.int32, (rows, LANES), 1)
    merged_ref[:, both:] = jnp.where(
        column == 0, high, jnp.where(column == 1, squares - high, 0.0)
    ).astype(jnp.bfloat16)


def down_rows(hidden_ref, near_ref, far_ref, finished_ref):
    half = hidden_ref.shape[0] // CORES
    chips, capacity, width = finished_ref.shape
    results = [
        lax.dot_general(
            hidden_ref[which * half : (which + 1) * half, :],
            weights[...],
            (((1,), (1,)), ((), ())),
            preferred_element_type=jnp.float32,
        ).reshape(chips, capacity // CORES, width)
        for which, weights in enumerate((near_ref, far_ref))
    ]
    finished_ref[...] = jnp.concatenate(results, axis=1).astype(jnp.bfloat16)


def exchange(values, axis, members):
    return lax.all_to_all(
        values, axis, split_axis=0, concat_axis=0, tiled=True, axis_index_groups=members
    )


def local(tokens, norm_gain, route_expert, route_gate, w_gate_up, w_down):
    tok_rows, width = tokens.shape
    groups = lax.axis_size("group")
    ways = lax.axis_size("slot")
    chips = groups // CORES
    picks = route_expert.shape[1]
    capacity = 2 * tok_rows * picks // groups
    slots = groups * capacity
    both = w_gate_up.shape[2]
    inner = both // 2
    columns = [
        [CORES * chip for chip in range(chips)],
        [CORES * chip + 1 for chip in reversed(range(chips))],
    ]
    swap = [(index, index ^ 1) for index in range(groups)]
    side = math.isqrt(ways)
    places = [
        [
            [group * ways + (side * b + a if group % CORES == 0 else side * a + b) for b in range(side)]
            for a in range(side)
        ]
        for group in range(groups)
    ]
    first_lines = [[line[b] for line in part] for part in places for b in range(side)]
    second_lines = [line for part in places for line in part]
    planes = [[place for line in part for place in line] for part in places]
    everywhere = ("group", "slot")

    rows, target = pl.pallas_call(
        functools.partial(place_rows, groups, capacity),
        out_shape=(
            jax.ShapeDtypeStruct((slots, width), jnp.bfloat16),
            jax.ShapeDtypeStruct((picks, tok_rows), jnp.int32),
        ),
        name="place_rows",
    )(route_expert.T, tokens.T)
    gates = route_gate.T
    row = lax.broadcasted_iota(jnp.int32, (slots, tok_rows), 0)
    weights_back = jnp.where(row == target[0:1], gates[0:1], 0) + jnp.where(
        row == target[1:2], gates[1:2], 0
    )

    arrived = exchange(rows.reshape(chips, CORES * capacity, width), "group", columns)
    gained = (w_gate_up[0].astype(jnp.float32) * norm_gain[:, None]).astype(jnp.bfloat16)
    other_gate = lax.ppermute(gained[:, :inner], "group", swap)
    other_up = lax.ppermute(gained[:, inner:], "group", swap)
    other_down = lax.ppermute(w_down, "group", swap)
    whole = pl.BlockSpec(memory_space=pltpu.VMEM)
    arrived, gained, other_gate, other_up, other_down, weights_back = lax.optimization_barrier(
        (arrived, gained, other_gate, other_up, other_down, weights_back)
    )

    def products(which, *weights):
        return pl.pallas_call(
            functools.partial(partial_rows, which),
            out_shape=jax.ShapeDtypeStruct((slots // CORES, both + LANES), jnp.bfloat16),
            in_specs=[whole] * (1 + len(weights)),
            out_specs=whole,
            compiler_params=pltpu.CompilerParams(vmem_limit_bytes=VMEM_BYTES),
            cost_estimate=pl.CostEstimate(
                flops=slots * width * both, bytes_accessed=4 * width * both, transcendentals=0
            ),
            name="partial_rows",
        )(arrived, *weights)

    sent = jnp.concatenate(
        [products(0, gained), products(1, other_gate, other_up)], axis=0
    )
    pieces = exchange(sent.reshape(side, slots // side, both + LANES), everywhere, first_lines)
    merged = pl.pallas_call(
        merge_rows,
        out_shape=jax.ShapeDtypeStruct((slots // side, both + LANES), jnp.bfloat16),
        in_specs=[whole],
        out_specs=whole,
        compiler_params=pltpu.CompilerParams(vmem_limit_bytes=VMEM_BYTES),
        name="merge_rows",
    )(pieces)
    pieces = exchange(merged.reshape(side, slots // ways, both + LANES), everywhere, second_lines)
    mine = jnp.sum(pieces.astype(jnp.float32), axis=0)
    scale = lax.rsqrt((mine[:, both : both + 1] + mine[:, both + 1 : both + 2]) / D + NORM_EPS)
    gate, up = mine[:, :inner] * scale, mine[:, inner:both] * scale
    hidden = (jax.nn.silu(gate) * up).astype(jnp.bfloat16)
    spread = exchange(jnp.broadcast_to(hidden[None], (ways,) + hidden.shape), everywhere, planes)
    finished = pl.pallas_call(
        down_rows,
        out_shape=jax.ShapeDtypeStruct((chips, CORES * capacity, width), jnp.bfloat16),
        in_specs=[whole] * 3,
        out_specs=whole,
        compiler_params=pltpu.CompilerParams(vmem_limit_bytes=VMEM_BYTES),
        cost_estimate=pl.CostEstimate(
            flops=2 * slots * width * inner, bytes_accessed=6 * width * inner, transcendentals=0
        ),
        name="down_rows",
    )(spread.reshape(slots, inner), w_down[0].T, other_down[0].T)
    returned = exchange(finished, "group", columns).reshape(slots, width)
    mixed = lax.dot_general(
        returned, weights_back, (((0,), (0,)), ((), ())), preferred_element_type=jnp.float32
    )
    return mixed.astype(jnp.bfloat16).T


def solution(mesh):
    placed = (
        P("group", "slot"),
        P("slot"),
        P("group", None),
        P("group", None),
        P("group", "slot", None),
        P("group", None, "slot"),
    )
    return jax.shard_map(
        local, mesh=mesh, in_specs=placed, out_specs=P("group", "slot"), check_vma=False
    )
```

```python
import functools
import math

import jax
import jax.numpy as jnp
from jax import lax
from jax.experimental import pallas as pl
from jax.experimental.pallas import tpu as pltpu
from jax.sharding import PartitionSpec as P

D = 7168


NORM_EPS = 1e-06
LANES = 128
STRIP = 512
STEP = 5
VMEM_BYTES = 32 * 1024 * 1024
CORES = 2


def place_rows(experts, capacity, routes_ref, tokens_ref, rows_ref, target_ref):
    slots = rows_ref.shape[0]
    count = tokens_ref.shape[1]
    chips = experts // CORES
    back = pow(STEP, -1, chips)
    core = lax.rem(lax.axis_index("group"), CORES)
    chosen = routes_ref[...]
    chosen = CORES * (((chosen >> 1) * back) & (chips - 1)) + (chosen & 1)
    chosen = jnp.where(core == 0, chosen, experts - 1 - chosen)
    first, second = chosen[0:1, :], chosen[1:2, :]
    names = lax.broadcasted_iota(jnp.int32, (experts, count), 0)
    one = (names == first).astype(jnp.float32)
    two = (names == second).astype(jnp.float32)
    earlier = lax.broadcasted_iota(jnp.int32, (count, count), 0) < lax.broadcasted_iota(
        jnp.int32, (count, count), 1
    )
    before = jnp.dot(
        (one + two).astype(jnp.bfloat16),
        earlier.astype(jnp.float32).astype(jnp.bfloat16),
        preferred_element_type=jnp.float32,
    )
    place_one = jnp.sum(one * before, axis=0, keepdims=True).astype(jnp.int32)
    place_two = jnp.sum(two * (before + one), axis=0, keepdims=True).astype(jnp.int32)
    slot_one, slot_two = first * capacity + place_one, second * capacity + place_two
    target_ref[0:1, :] = slot_one
    target_ref[1:2, :] = slot_two
    row = lax.broadcasted_iota(jnp.int32, (slots, count), 0)
    picked = jnp.where((row == slot_one) | (row == slot_two), 1.0, 0.0).astype(jnp.bfloat16)
    rows_ref[...] = lax.dot_general(
        picked, tokens_ref[...], (((1,), (1,)), ((), ())), preferred_element_type=jnp.float32
    ).astype(jnp.bfloat16)


def partial_rows(which, arrived_ref, *refs):
    weights, sent_ref = refs[:-1], refs[-1]
    half, columns = sent_ref.shape
    both = columns - LANES
    values = arrived_ref[...].astype(jnp.float32)
    capacity = values.shape[1] // CORES
    column = lax.broadcasted_iota(jnp.int32, (half, LANES), 1)
    mine = values[:, which * capacity : (which + 1) * capacity].reshape(half, -1)
    exact = mine.astype(jnp.bfloat16)
    squares = jnp.sum(mine * mine, axis=1, keepdims=True)
    high = squares.astype(jnp.bfloat16).astype(jnp.float32)
    sent_ref[:, both:] = jnp.where(
        column == 0, high, jnp.where(column == 1, squares - high, 0.0)
    ).astype(jnp.bfloat16)
    done = 0
    for part in weights:
        for start in range(0, part.shape[1], STRIP):
            sent_ref[:, done : done + STRIP] = jnp.dot(
                exact, part[:, start : start + STRIP], preferred_element_type=jnp.float32
            ).astype(jnp.bfloat16)
            done += STRIP


def merge_rows(pieces_ref, merged_ref):
    rows, columns = merged_ref.shape
    both = columns - LANES
    for start in range(0, both, STRIP):
        strip = slice(start, start + STRIP)
        merged_ref[:, strip] = jnp.sum(pieces_ref[:, :, strip].astype(jnp.float32), axis=0).astype(
            jnp.bfloat16
        )
    tail = jnp.sum(pieces_ref[:, :, both:].astype(jnp.float32), axis=0)
    squares = tail[:, 0:1] + tail[:, 1:2]
    high = squares.astype(jnp.bfloat16).astype(jnp.float32)
    column = lax.broadcasted_iota(jnp.int32, (rows, LANES), 1)
    merged_ref[:, both:] = jnp.where(
        column == 0, high, jnp.where(column == 1, squares - high, 0.0)
    ).astype(jnp.bfloat16)


def down_rows(hidden_ref, near_ref, far_ref, finished_ref):
    half = hidden_ref.shape[0] // CORES
    chips, capacity, width = finished_ref.shape
    results = [
        lax.dot_general(
            hidden_ref[which * half : (which + 1) * half, :],
            weights[...],
            (((1,), (1,)), ((), ())),
            preferred_element_type=jnp.float32,
        ).reshape(chips, capacity // CORES, width)
        for which, weights in enumerate((near_ref, far_ref))
    ]
    finished_ref[...] = jnp.concatenate(results, axis=1).astype(jnp.bfloat16)


def exchange(values, axis, members):
    return lax.all_to_all(
        values, axis, split_axis=0, concat_axis=0, tiled=True, axis_index_groups=members
    )


def local(tokens, norm_gain, route_expert, route_gate, w_gate_up, w_down):
    tok_rows, width = tokens.shape
    groups = lax.axis_size("group")
    ways = lax.axis_size("slot")
    chips = groups // CORES
    picks = route_expert.shape[1]
    capacity = 2 * tok_rows * picks // groups
    slots = groups * capacity
    both = w_gate_up.shape[2]
    inner = both // 2
    listed = [STEP * place % chips for place in range(chips)]
    columns = [
        [CORES * chip for chip in listed],
        [CORES * chip + 1 for chip in reversed(listed)],
    ]
    swap = [(index, index ^ 1) for index in range(groups)]
    side = math.isqrt(ways)
    places = [
        [
            [group * ways + (side * b + a if group % CORES == 0 else side * a + b) for b in range(side)]
            for a in range(side)
        ]
        for group in range(groups)
    ]
    first_lines = [[line[b] for line in part] for part in places for b in range(side)]
    second_lines = [line for part in places for line in part]
    planes = [[place for line in part for place in line] for part in places]
    everywhere = ("group", "slot")

    rows, target = pl.pallas_call(
        functools.partial(place_rows, groups, capacity),
        out_shape=(
            jax.ShapeDtypeStruct((slots, width), jnp.bfloat16),
            jax.ShapeDtypeStruct((picks, tok_rows), jnp.int32),
        ),
        name="place_rows",
    )(route_expert.T, tokens.T)
    gates = route_gate.T
    row = lax.broadcasted_iota(jnp.int32, (slots, tok_rows), 0)
    weights_back = jnp.where(row == target[0:1], gates[0:1], 0) + jnp.where(
        row == target[1:2], gates[1:2], 0
    )

    arrived = exchange(rows.reshape(chips, CORES * capacity, width), "group", columns)
    gained = (w_gate_up[0].astype(jnp.float32) * norm_gain[:, None]).astype(jnp.bfloat16)
    other_gate = lax.ppermute(gained[:, :inner], "group", swap)
    other_up = lax.ppermute(gained[:, inner:], "group", swap)
    other_down = lax.ppermute(w_down, "group", swap)
    whole = pl.BlockSpec(memory_space=pltpu.VMEM)
    arrived, gained, other_gate, other_up, other_down, weights_back = lax.optimization_barrier(
        (arrived, gained, other_gate, other_up, other_down, weights_back)
    )

    def products(which, *weights):
        return pl.pallas_call(
            functools.partial(partial_rows, which),
            out_shape=jax.ShapeDtypeStruct((slots // CORES, both + LANES), jnp.bfloat16),
            in_specs=[whole] * (1 + len(weights)),
            out_specs=whole,
            compiler_params=pltpu.CompilerParams(vmem_limit_bytes=VMEM_BYTES),
            cost_estimate=pl.CostEstimate(
                flops=slots * width * both, bytes_accessed=4 * width * both, transcendentals=0
            ),
            name="partial_rows",
        )(arrived, *weights)

    sent = jnp.concatenate(
        [products(0, gained), products(1, other_gate, other_up)], axis=0
    )
    pieces = exchange(sent.reshape(side, slots // side, both + LANES), everywhere, first_lines)
    merged = pl.pallas_call(
        merge_rows,
        out_shape=jax.ShapeDtypeStruct((slots // side, both + LANES), jnp.bfloat16),
        in_specs=[whole],
        out_specs=whole,
        compiler_params=pltpu.CompilerParams(vmem_limit_bytes=VMEM_BYTES),
        name="merge_rows",
    )(pieces)
    pieces = exchange(merged.reshape(side, slots // ways, both + LANES), everywhere, second_lines)
    mine = jnp.sum(pieces.astype(jnp.float32), axis=0)
    scale = lax.rsqrt((mine[:, both : both + 1] + mine[:, both + 1 : both + 2]) / D + NORM_EPS)
    gate, up = mine[:, :inner] * scale, mine[:, inner:both] * scale
    hidden = (jax.nn.silu(gate) * up).astype(jnp.bfloat16)
    spread = exchange(jnp.broadcast_to(hidden[None], (ways,) + hidden.shape), everywhere, planes)
    finished = pl.pallas_call(
        down_rows,
        out_shape=jax.ShapeDtypeStruct((chips, CORES * capacity, width), jnp.bfloat16),
        in_specs=[whole] * 3,
        out_specs=whole,
        compiler_params=pltpu.CompilerParams(vmem_limit_bytes=VMEM_BYTES),
        cost_estimate=pl.CostEstimate(
            flops=2 * slots * width * inner, bytes_accessed=6 * width * inner, transcendentals=0
        ),
        name="down_rows",
    )(spread.reshape(slots, inner), w_down[0].T, other_down[0].T)
    returned = exchange(finished, "group", columns).reshape(slots, width)
    mixed = lax.dot_general(
        returned, weights_back, (((0,), (0,)), ((), ())), preferred_element_type=jnp.float32
    )
    return mixed.astype(jnp.bfloat16).T


def solution(mesh):
    placed = (
        P("group", "slot"),
        P("slot"),
        P("group", None),
        P("group", None),
        P("group", "slot", None),
        P("group", None, "slot"),
    )
    return jax.shard_map(
        local, mesh=mesh, in_specs=placed, out_specs=P("group", "slot"), check_vma=False
    )
```

```python
import functools
import math

import jax
import jax.numpy as jnp
from jax import lax
from jax.experimental import pallas as pl
from jax.experimental.pallas import tpu as pltpu
from jax.sharding import PartitionSpec as P

D = 7168


NORM_EPS = 1e-06
LANES = 128
STRIP = 512
STEP = 15
VMEM_BYTES = 32 * 1024 * 1024
CORES = 2


def place_rows(experts, capacity, routes_ref, tokens_ref, rows_ref, target_ref):
    slots = rows_ref.shape[0]
    count = tokens_ref.shape[1]
    chips = experts // CORES
    back = pow(STEP, -1, chips)
    core = lax.rem(lax.axis_index("group"), CORES)
    chosen = routes_ref[...]
    chosen = CORES * (((chosen >> 1) * back) & (chips - 1)) + (chosen & 1)
    chosen = jnp.where(core == 0, chosen, experts - 1 - chosen)
    first, second = chosen[0:1, :], chosen[1:2, :]
    names = lax.broadcasted_iota(jnp.int32, (experts, count), 0)
    one = (names == first).astype(jnp.float32)
    two = (names == second).astype(jnp.float32)
    earlier = lax.broadcasted_iota(jnp.int32, (count, count), 0) < lax.broadcasted_iota(
        jnp.int32, (count, count), 1
    )
    before = jnp.dot(
        (one + two).astype(jnp.bfloat16),
        earlier.astype(jnp.float32).astype(jnp.bfloat16),
        preferred_element_type=jnp.float32,
    )
    place_one = jnp.sum(one * before, axis=0, keepdims=True).astype(jnp.int32)
    place_two = jnp.sum(two * (before + one), axis=0, keepdims=True).astype(jnp.int32)
    slot_one, slot_two = first * capacity + place_one, second * capacity + place_two
    target_ref[0:1, :] = slot_one
    target_ref[1:2, :] = slot_two
    row = lax.broadcasted_iota(jnp.int32, (slots, count), 0)
    picked = jnp.where((row == slot_one) | (row == slot_two), 1.0, 0.0).astype(jnp.bfloat16)
    rows_ref[...] = lax.dot_general(
        picked, tokens_ref[...], (((1,), (1,)), ((), ())), preferred_element_type=jnp.float32
    ).astype(jnp.bfloat16)


def partial_rows(which, arrived_ref, *refs):
    weights, sent_ref = refs[:-1], refs[-1]
    half, columns = sent_ref.shape
    both = columns - LANES
    values = arrived_ref[...].astype(jnp.float32)
    capacity = values.shape[1] // CORES
    column = lax.broadcasted_iota(jnp.int32, (half, LANES), 1)
    mine = values[:, which * capacity : (which + 1) * capacity].reshape(half, -1)
    exact = mine.astype(jnp.bfloat16)
    squares = jnp.sum(mine * mine, axis=1, keepdims=True)
    high = squares.astype(jnp.bfloat16).astype(jnp.float32)
    sent_ref[:, both:] = jnp.where(
        column == 0, high, jnp.where(column == 1, squares - high, 0.0)
    ).astype(jnp.bfloat16)
    done = 0
    for part in weights:
        for start in range(0, part.shape[1], STRIP):
            sent_ref[:, done : done + STRIP] = jnp.dot(
                exact, part[:, start : start + STRIP], preferred_element_type=jnp.float32
            ).astype(jnp.bfloat16)
            done += STRIP


def merge_rows(pieces_ref, merged_ref):
    rows, columns = merged_ref.shape
    both = columns - LANES
    for start in range(0, both, STRIP):
        strip = slice(start, start + STRIP)
        merged_ref[:, strip] = jnp.sum(pieces_ref[:, :, strip].astype(jnp.float32), axis=0).astype(
            jnp.bfloat16
        )
    tail = jnp.sum(pieces_ref[:, :, both:].astype(jnp.float32), axis=0)
    squares = tail[:, 0:1] + tail[:, 1:2]
    high = squares.astype(jnp.bfloat16).astype(jnp.float32)
    column = lax.broadcasted_iota(jnp.int32, (rows, LANES), 1)
    merged_ref[:, both:] = jnp.where(
        column == 0, high, jnp.where(column == 1, squares - high, 0.0)
    ).astype(jnp.bfloat16)


def down_rows(hidden_ref, near_ref, far_ref, finished_ref):
    half = hidden_ref.shape[0] // CORES
    chips, capacity, width = finished_ref.shape
    results = [
        lax.dot_general(
            hidden_ref[which * half : (which + 1) * half, :],
            weights[...],
            (((1,), (1,)), ((), ())),
            preferred_element_type=jnp.float32,
        ).reshape(chips, capacity // CORES, width)
        for which, weights in enumerate((near_ref, far_ref))
    ]
    finished_ref[...] = jnp.concatenate(results, axis=1).astype(jnp.bfloat16)


def exchange(values, axis, members):
    return lax.all_to_all(
        values, axis, split_axis=0, concat_axis=0, tiled=True, axis_index_groups=members
    )


def local(tokens, norm_gain, route_expert, route_gate, w_gate_up, w_down):
    tok_rows, width = tokens.shape
    groups = lax.axis_size("group")
    ways = lax.axis_size("slot")
    chips = groups // CORES
    picks = route_expert.shape[1]
    capacity = 2 * tok_rows * picks // groups
    slots = groups * capacity
    both = w_gate_up.shape[2]
    inner = both // 2
    listed = [STEP * place % chips for place in range(chips)]
    columns = [
        [CORES * chip for chip in listed],
        [CORES * chip + 1 for chip in reversed(listed)],
    ]
    swap = [(index, index ^ 1) for index in range(groups)]
    side = math.isqrt(ways)
    places = [
        [
            [group * ways + (side * b + a if group % CORES == 0 else side * a + b) for b in range(side)]
            for a in range(side)
        ]
        for group in range(groups)
    ]
    first_lines = [[line[b] for line in part] for part in places for b in range(side)]
    second_lines = [line for part in places for line in part]
    planes = [[place for line in part for place in line] for part in places]
    everywhere = ("group", "slot")

    rows, target = pl.pallas_call(
        functools.partial(place_rows, groups, capacity),
        out_shape=(
            jax.ShapeDtypeStruct((slots, width), jnp.bfloat16),
            jax.ShapeDtypeStruct((picks, tok_rows), jnp.int32),
        ),
        name="place_rows",
    )(route_expert.T, tokens.T)
    gates = route_gate.T
    row = lax.broadcasted_iota(jnp.int32, (slots, tok_rows), 0)
    weights_back = jnp.where(row == target[0:1], gates[0:1], 0) + jnp.where(
        row == target[1:2], gates[1:2], 0
    )

    arrived = exchange(rows.reshape(chips, CORES * capacity, width), "group", columns)
    gained = (w_gate_up[0].astype(jnp.float32) * norm_gain[:, None]).astype(jnp.bfloat16)
    other_gate = lax.ppermute(gained[:, :inner], "group", swap)
    other_up = lax.ppermute(gained[:, inner:], "group", swap)
    other_down = lax.ppermute(w_down, "group", swap)
    whole = pl.BlockSpec(memory_space=pltpu.VMEM)
    arrived, gained, other_gate, other_up, other_down, weights_back = lax.optimization_barrier(
        (arrived, gained, other_gate, other_up, other_down, weights_back)
    )

    def products(which, *weights):
        return pl.pallas_call(
            functools.partial(partial_rows, which),
            out_shape=jax.ShapeDtypeStruct((slots // CORES, both + LANES), jnp.bfloat16),
            in_specs=[whole] * (1 + len(weights)),
            out_specs=whole,
            compiler_params=pltpu.CompilerParams(vmem_limit_bytes=VMEM_BYTES),
            cost_estimate=pl.CostEstimate(
                flops=slots * width * both, bytes_accessed=4 * width * both, transcendentals=0
            ),
            name="partial_rows",
        )(arrived, *weights)

    sent = jnp.concatenate(
        [products(0, gained), products(1, other_gate, other_up)], axis=0
    )
    pieces = exchange(sent.reshape(side, slots // side, both + LANES), everywhere, first_lines)
    merged = pl.pallas_call(
        merge_rows,
        out_shape=jax.ShapeDtypeStruct((slots // side, both + LANES), jnp.bfloat16),
        in_specs=[whole],
        out_specs=whole,
        compiler_params=pltpu.CompilerParams(vmem_limit_bytes=VMEM_BYTES),
        name="merge_rows",
    )(pieces)
    pieces = exchange(merged.reshape(side, slots // ways, both + LANES), everywhere, second_lines)
    mine = jnp.sum(pieces.astype(jnp.float32), axis=0)
    scale = lax.rsqrt((mine[:, both : both + 1] + mine[:, both + 1 : both + 2]) / D + NORM_EPS)
    gate, up = mine[:, :inner] * scale, mine[:, inner:both] * scale
    hidden = (jax.nn.silu(gate) * up).astype(jnp.bfloat16)
    spread = exchange(jnp.broadcast_to(hidden[None], (ways,) + hidden.shape), everywhere, planes)
    finished = pl.pallas_call(
        down_rows,
        out_shape=jax.ShapeDtypeStruct((chips, CORES * capacity, width), jnp.bfloat16),
        in_specs=[whole] * 3,
        out_specs=whole,
        compiler_params=pltpu.CompilerParams(vmem_limit_bytes=VMEM_BYTES),
        cost_estimate=pl.CostEstimate(
            flops=2 * slots * width * inner, bytes_accessed=6 * width * inner, transcendentals=0
        ),
        name="down_rows",
    )(spread.reshape(slots, inner), w_down[0].T, other_down[0].T)
    returned = exchange(finished, "group", columns).reshape(slots, width)
    mixed = lax.dot_general(
        returned, weights_back, (((0,), (0,)), ((), ())), preferred_element_type=jnp.float32
    )
    return mixed.astype(jnp.bfloat16).T


def solution(mesh):
    placed = (
        P("group", "slot"),
        P("slot"),
        P("group", None),
        P("group", None),
        P("group", "slot", None),
        P("group", None, "slot"),
    )
    return jax.shard_map(
        local, mesh=mesh, in_specs=placed, out_specs=P("group", "slot"), check_vma=False
    )
```

```python
import functools
import math

import jax
import jax.numpy as jnp
from jax import lax
from jax.experimental import pallas as pl
from jax.experimental.pallas import tpu as pltpu
from jax.sharding import PartitionSpec as P

D = 7168


NORM_EPS = 1e-06
LANES = 128
STRIP = 512
STEP = 15
VMEM_BYTES = 32 * 1024 * 1024
CORES = 2


def place_rows(experts, capacity, routes_ref, tokens_ref, rows_ref, target_ref):
    slots = rows_ref.shape[0]
    count = tokens_ref.shape[1]
    chips = experts // CORES
    back = pow(STEP, -1, chips)
    core = lax.rem(lax.axis_index("group"), CORES)
    chosen = routes_ref[...]
    chosen = CORES * (((chosen >> 1) * back) & (chips - 1)) + (chosen & 1)
    chosen = jnp.where(core == 0, chosen, experts - 1 - chosen)
    first, second = chosen[0:1, :], chosen[1:2, :]
    names = lax.broadcasted_iota(jnp.int32, (experts, count), 0)
    one = (names == first).astype(jnp.float32)
    two = (names == second).astype(jnp.float32)
    earlier = lax.broadcasted_iota(jnp.int32, (count, count), 0) < lax.broadcasted_iota(
        jnp.int32, (count, count), 1
    )
    before = jnp.dot(
        (one + two).astype(jnp.bfloat16),
        earlier.astype(jnp.float32).astype(jnp.bfloat16),
        preferred_element_type=jnp.float32,
    )
    place_one = jnp.sum(one * before, axis=0, keepdims=True).astype(jnp.int32)
    place_two = jnp.sum(two * (before + one), axis=0, keepdims=True).astype(jnp.int32)
    slot_one, slot_two = first * capacity + place_one, second * capacity + place_two
    target_ref[0:1, :] = slot_one
    target_ref[1:2, :] = slot_two
    row = lax.broadcasted_iota(jnp.int32, (slots, count), 0)
    picked = jnp.where((row == slot_one) | (row == slot_two), 1.0, 0.0).astype(jnp.bfloat16)
    rows_ref[...] = lax.dot_general(
        picked, tokens_ref[...], (((1,), (1,)), ((), ())), preferred_element_type=jnp.float32
    ).astype(jnp.bfloat16)


def partial_rows(which, arrived_ref, *refs):
    weights, sent_ref = refs[:-1], refs[-1]
    half, columns = sent_ref.shape
    both = columns - LANES
    values = arrived_ref[...].astype(jnp.float32)
    capacity = values.shape[1] // CORES
    column = lax.broadcasted_iota(jnp.int32, (half, LANES), 1)
    mine = values[:, which * capacity : (which + 1) * capacity].reshape(half, -1)
    exact = mine.astype(jnp.bfloat16)
    squares = jnp.sum(mine * mine, axis=1, keepdims=True)
    high = squares.astype(jnp.bfloat16).astype(jnp.float32)
    sent_ref[:, both:] = jnp.where(
        column == 0, high, jnp.where(column == 1, squares - high, 0.0)
    ).astype(jnp.bfloat16)
    done = 0
    for part in weights:
        for start in range(0, part.shape[1], STRIP):
            sent_ref[:, done : done + STRIP] = jnp.dot(
                exact, part[:, start : start + STRIP], preferred_element_type=jnp.float32
            ).astype(jnp.bfloat16)
            done += STRIP


def merge_rows(pieces_ref, merged_ref):
    rows, columns = merged_ref.shape
    both = columns - LANES
    for start in range(0, both, STRIP):
        strip = slice(start, start + STRIP)
        merged_ref[:, strip] = jnp.sum(pieces_ref[:, :, strip].astype(jnp.float32), axis=0).astype(
            jnp.bfloat16
        )
    tail = jnp.sum(pieces_ref[:, :, both:].astype(jnp.float32), axis=0)
    squares = tail[:, 0:1] + tail[:, 1:2]
    high = squares.astype(jnp.bfloat16).astype(jnp.float32)
    column = lax.broadcasted_iota(jnp.int32, (rows, LANES), 1)
    merged_ref[:, both:] = jnp.where(
        column == 0, high, jnp.where(column == 1, squares - high, 0.0)
    ).astype(jnp.bfloat16)


def down_rows(hidden_ref, near_ref, far_ref, finished_ref):
    half = hidden_ref.shape[0] // CORES
    chips, capacity, width = finished_ref.shape
    results = [
        lax.dot_general(
            hidden_ref[which * half : (which + 1) * half, :],
            weights[...],
            (((1,), (1,)), ((), ())),
            preferred_element_type=jnp.float32,
        ).reshape(chips, capacity // CORES, width)
        for which, weights in enumerate((near_ref, far_ref))
    ]
    finished_ref[...] = jnp.concatenate(results, axis=1).astype(jnp.bfloat16)


def exchange(values, axis, members):
    return lax.all_to_all(
        values, axis, split_axis=0, concat_axis=0, tiled=True, axis_index_groups=members
    )


def local(tokens, norm_gain, route_expert, route_gate, w_gate_up, w_down):
    tok_rows, width = tokens.shape
    groups = lax.axis_size("group")
    ways = lax.axis_size("slot")
    chips = groups // CORES
    picks = route_expert.shape[1]
    capacity = 2 * tok_rows * picks // groups
    slots = groups * capacity
    both = w_gate_up.shape[2]
    inner = both // 2
    listed = [STEP * place % chips for place in range(chips)]
    columns = [
        [CORES * chip for chip in listed],
        [CORES * chip + 1 for chip in reversed(listed)],
    ]
    swap = [(index, index ^ 1) for index in range(groups)]
    side = math.isqrt(ways)
    places = [
        [
            [group * ways + (side * b + a if group % CORES == 0 else ways - 1 - side * a - b) for b in range(side)]
            for a in range(side)
        ]
        for group in range(groups)
    ]
    first_lines = [[line[b] for line in part] for part in places for b in range(side)]
    second_lines = [line for part in places for line in part]
    planes = [[place for line in part for place in line] for part in places]
    everywhere = ("group", "slot")

    rows, target = pl.pallas_call(
        functools.partial(place_rows, groups, capacity),
        out_shape=(
            jax.ShapeDtypeStruct((slots, width), jnp.bfloat16),
            jax.ShapeDtypeStruct((picks, tok_rows), jnp.int32),
        ),
        name="place_rows",
    )(route_expert.T, tokens.T)
    gates = route_gate.T
    row = lax.broadcasted_iota(jnp.int32, (slots, tok_rows), 0)
    weights_back = jnp.where(row == target[0:1], gates[0:1], 0) + jnp.where(
        row == target[1:2], gates[1:2], 0
    )

    arrived = exchange(rows.reshape(chips, CORES * capacity, width), "group", columns)
    gained = (w_gate_up[0].astype(jnp.float32) * norm_gain[:, None]).astype(jnp.bfloat16)
    other_gate = lax.ppermute(gained[:, :inner], "group", swap)
    other_up = lax.ppermute(gained[:, inner:], "group", swap)
    other_down = lax.ppermute(w_down, "group", swap)
    whole = pl.BlockSpec(memory_space=pltpu.VMEM)
    arrived, gained, other_gate, other_up, other_down, weights_back = lax.optimization_barrier(
        (arrived, gained, other_gate, other_up, other_down, weights_back)
    )

    def products(which, *weights):
        return pl.pallas_call(
            functools.partial(partial_rows, which),
            out_shape=jax.ShapeDtypeStruct((slots // CORES, both + LANES), jnp.bfloat16),
            in_specs=[whole] * (1 + len(weights)),
            out_specs=whole,
            compiler_params=pltpu.CompilerParams(vmem_limit_bytes=VMEM_BYTES),
            cost_estimate=pl.CostEstimate(
                flops=slots * width * both, bytes_accessed=4 * width * both, transcendentals=0
            ),
            name="partial_rows",
        )(arrived, *weights)

    sent = jnp.concatenate(
        [products(0, gained), products(1, other_gate, other_up)], axis=0
    )
    pieces = exchange(sent.reshape(side, slots // side, both + LANES), everywhere, first_lines)
    merged = pl.pallas_call(
        merge_rows,
        out_shape=jax.ShapeDtypeStruct((slots // side, both + LANES), jnp.bfloat16),
        in_specs=[whole],
        out_specs=whole,
        compiler_params=pltpu.CompilerParams(vmem_limit_bytes=VMEM_BYTES),
        name="merge_rows",
    )(pieces)
    pieces = exchange(merged.reshape(side, slots // ways, both + LANES), everywhere, second_lines)
    mine = jnp.sum(pieces.astype(jnp.float32), axis=0)
    scale = lax.rsqrt((mine[:, both : both + 1] + mine[:, both + 1 : both + 2]) / D + NORM_EPS)
    gate, up = mine[:, :inner] * scale, mine[:, inner:both] * scale
    hidden = (jax.nn.silu(gate) * up).astype(jnp.bfloat16)
    spread = exchange(jnp.broadcast_to(hidden[None], (ways,) + hidden.shape), everywhere, planes)
    finished = pl.pallas_call(
        down_rows,
        out_shape=jax.ShapeDtypeStruct((chips, CORES * capacity, width), jnp.bfloat16),
        in_specs=[whole] * 3,
        out_specs=whole,
        compiler_params=pltpu.CompilerParams(vmem_limit_bytes=VMEM_BYTES),
        cost_estimate=pl.CostEstimate(
            flops=2 * slots * width * inner, bytes_accessed=6 * width * inner, transcendentals=0
        ),
        name="down_rows",
    )(spread.reshape(slots, inner), w_down[0].T, other_down[0].T)
    returned = exchange(finished, "group", columns).reshape(slots, width)
    mixed = lax.dot_general(
        returned, weights_back, (((0,), (0,)), ((), ())), preferred_element_type=jnp.float32
    )
    return mixed.astype(jnp.bfloat16).T


def solution(mesh):
    placed = (
        P("group", "slot"),
        P("slot"),
        P("group", None),
        P("group", None),
        P("group", "slot", None),
        P("group", None, "slot"),
    )
    return jax.shard_map(
        local, mesh=mesh, in_specs=placed, out_specs=P("group", "slot"), check_vma=False
    )
```
